32 devices in a mesh: fsdp: 4 (over z), seq: 8 (over y, x, core).
Axes of the slice: x: 2, y: 2, z: 4, core: 2. Of those that a mesh axis runs over, the one named last changes fastest.
Arguments:
- tokens: bfloat16 [1792, 4096], P(('fsdp', 'seq')), may hold values from -6 to 6
- grad_out: bfloat16 [1792, 4096], P(('fsdp', 'seq')), may hold values from -6 to 6
- gate_weight: bfloat16 [4096, 14336], P('fsdp', 'seq'), may hold values from -0.09375 to 0.09375
- up_weight: bfloat16 [4096, 14336], P('fsdp', 'seq'), may hold values from -0.09375 to 0.09375
- down_weight: bfloat16 [14336, 4096], P('seq', 'fsdp'), may hold values from -0.09375 to 0.09375
- keep_mask: int32 [8, 112], P(None, 'seq'), may hold values from 0 to 1, as said below
- task_ids: int32 [1792], P('fsdp'), may hold values from 0 to 7
Outputs:
- layer_out: bfloat16 [1792, 4096], P(('fsdp', 'seq'))
- input_grad: bfloat16 [1792, 4096], P(('fsdp', 'seq'))
The draws below stay inside these ranges and needn't reach their ends.
Inputs may be any that keep to these rules, and one draw needn't show every extreme that they name: `keep_mask`: entries are 0 or 1. In each aligned group of 14 consecutive blocks at most 8 blocks are kept by some task, and exactly 8 in at least one group; the other blocks of a group are kept by no task.
All inputs are finite; a program needn't handle non-finite values.
Results may differ from the reference program's by a relative error of at most 0.014.
Values may be sent and summed in bfloat16 or wider, within the bound.
No kernel may reach another device: no remote copies, remote signals or barrier semaphores. Data moves between devices by JAX's collectives and lax.ppermute only.
A program may use at most 128 MiB of HBM per device.

```python
import jax
import jax.numpy as jnp
from jax import lax

D = 4096
FF = 14336
BLOCK = 128
NTASK = 8
TOKENS = 1792
NB = 112
NB_LOC = 14
LIVE_LOC = 8
N_SEQ = 8


def draw_keep_mask(key, part):
    groups = NB // NB_LOC
    keys = jax.random.split(key, 6)
    counts = jax.random.randint(keys[0], (groups,), (LIVE_LOC + 1) // 2, LIVE_LOC + 1)
    full_group = jax.random.randint(keys[1], (), 0, groups)
    counts = jnp.where(jnp.arange(groups, dtype=jnp.int32) == full_group, LIVE_LOC, counts)
    shuffled = jax.vmap(lambda single: jax.random.permutation(single, NB_LOC))(jax.random.split(keys[2], groups))
    positions = jnp.argsort(shuffled, axis=1)
    live_blocks = (positions < counts[:, None]).reshape(NB)
    thresholds = jax.random.randint(keys[3], (NTASK, 1), 1, 10)
    dice_rolls = jax.random.randint(keys[4], (NTASK, NB), 0, 10)
    kept_blocks = dice_rolls < thresholds
    owner_task = jax.random.randint(keys[5], (NB,), 0, NTASK)
    kept_blocks = kept_blocks | (jnp.arange(NTASK, dtype=jnp.int32)[:, None] == owner_task[None, :])
    return (kept_blocks & live_blocks[None, :]).astype(jnp.int32)


def set_ends(entries, key, low, high):
    shape = entries.shape
    index_at = [jax.random.randint(jax.random.fold_in(key, axis), (), 0, shape[axis]) for axis in range(len(shape))]
    entries = entries.at[tuple(index_at)].set(low)
    longest = shape.index(max(shape))
    index_at[longest] = (index_at[longest] + 1) % shape[longest]
    return entries.at[tuple(index_at)].set(high)


def levels(key, dims, shards, low, high):
    def one(position, parts):
        heights = jax.random.uniform(jax.random.fold_in(jax.random.fold_in(key, 6), position), (parts,), jnp.float32, low / len(shards), high / len(shards))
        return jnp.repeat(jnp.exp(heights), dims[position] // parts).reshape((-1,) + (1,) * (len(dims) - position - 1))

    gain = one(*shards[0])
    for cut in shards[1:]:
        gain = gain * one(*cut)
    return gain


def normal_values(own_key, shape, width, limit, shards=(), kind=jnp.bfloat16):
    values = width * jax.random.normal(own_key, shape, jnp.float32)
    if shards:
        values = values * levels(own_key, shape, shards, -0.22, 0.18)
    return jnp.clip(values, -limit, limit).astype(kind)


def setup_inputs(seed: int = 0) -> dict:
    arg_keys = jax.random.split(jax.random.key(seed), 8)
    tokens = normal_values(arg_keys[0], (TOKENS, D), 1.0, 6.0, ((0, 32),))
    grad_out = normal_values(arg_keys[1], (TOKENS, D), 1.0, 6.0, ((0, 32),))
    gate_weight = normal_values(arg_keys[2], (D, FF), D ** -0.5, 0.09375, ((0, 4), (1, 8)))
    up_weight = normal_values(arg_keys[3], (D, FF), D ** -0.5, 0.09375, ((0, 4), (1, 8)))
    down_weight = normal_values(arg_keys[4], (FF, D), (FF // 4) ** -0.5, 0.09375, ((0, 8), (1, 4)))
    keep_mask = draw_keep_mask(jax.random.fold_in(arg_keys[7], 71), 0)
    task_ids = set_ends(jax.random.randint(arg_keys[6], (TOKENS,), 0, NTASK), jax.random.fold_in(arg_keys[6], 1), 0, NTASK - 1).astype(jnp.int32)
    return {"tokens": tokens, "grad_out": grad_out, "gate_weight": gate_weight, "up_weight": up_weight, "down_weight": down_weight, "keep_mask": keep_mask, "task_ids": task_ids}


def transposed(left, right):
    return lax.dot_general(left, right, (((1,), (1,)), ((), ())), preferred_element_type=jnp.float32)


def reference(tokens, grad_out, gate_weight, up_weight, down_weight, keep_mask, task_ids):
    onehot_tasks = (task_ids[:, None] == jnp.arange(NTASK, dtype=jnp.int32)[None, :]).astype(jnp.float32)
    row_keep = jnp.dot(onehot_tasks, keep_mask.astype(jnp.float32))
    neuron_mask = jnp.repeat(row_keep, BLOCK, axis=1)
    gate_pre = jnp.dot(tokens, gate_weight, preferred_element_type=jnp.float32)
    up_pre = jnp.dot(tokens, up_weight, preferred_element_type=jnp.float32)
    logistic = jax.nn.sigmoid(gate_pre)
    activated = gate_pre * logistic
    hidden = (activated * up_pre * neuron_mask).astype(jnp.bfloat16)
    hidden_grad = transposed(grad_out, down_weight)
    masked_grad = hidden_grad * neuron_mask
    gate_grad = (masked_grad * up_pre * logistic * (1.0 + gate_pre * (1.0 - logistic))).astype(jnp.bfloat16)
    up_grad = (masked_grad * activated).astype(jnp.bfloat16)
    group_width = FF // N_SEQ

    def add_group(totals, group):
        start = (group * group_width).astype(jnp.int32)
        hidden_piece = lax.dynamic_slice_in_dim(hidden, start, group_width, 1)
        down_piece = lax.dynamic_slice_in_dim(down_weight, start, group_width, 0)
        gate_piece = lax.dynamic_slice_in_dim(gate_grad, start, group_width, 1)
        up_piece = lax.dynamic_slice_in_dim(up_grad, start, group_width, 1)
        gate_cols = lax.dynamic_slice_in_dim(gate_weight, start, group_width, 1)
        up_cols = lax.dynamic_slice_in_dim(up_weight, start, group_width, 1)
        out_part = jnp.dot(hidden_piece, down_piece, preferred_element_type=jnp.float32).astype(jnp.bfloat16)
        grad_part = (transposed(gate_piece, gate_cols) + transposed(up_piece, up_cols)).astype(jnp.bfloat16)
        out_part, grad_part = lax.optimization_barrier((out_part, grad_part))
        return (totals[0] + out_part.astype(jnp.float32), totals[1] + grad_part.astype(jnp.float32)), None

    empty = jnp.zeros((tokens.shape[0], D), jnp.float32)
    sums, unused = lax.scan(add_group, (empty, empty), jnp.arange(N_SEQ, dtype=jnp.int32))
    return sums[0].astype(jnp.bfloat16), sums[1].astype(jnp.bfloat16)
```

```python
import functools

import jax
import jax.numpy as jnp
from jax import lax
from jax.experimental import pallas as pl
from jax.experimental.pallas import tpu as pltpu
from jax.sharding import PartitionSpec as P

BF16, F32 = jnp.bfloat16, jnp.float32


def dot_t(left, right):
    return lax.dot_general(left, right, (((1,), (1,)), ((), ())), preferred_element_type=F32)


def dot(left, right):
    return jnp.dot(left, right, preferred_element_type=F32)


def pick_kernel(nf, kept, width, layer_ref, keep_ref, gate, up, down, *rest):
    sends, (down_out, keep_out) = rest[:nf], rest[nf : nf + 2]
    chosen, stage, down_stage, in_sems, out_sems = rest[nf + 2 :]
    tasks, blocks = keep_ref.shape
    for slot in range(kept):
        chosen[slot] = 0
    live = jnp.int32(0)
    flags = []
    for b in range(blocks):
        alive = keep_ref[0, b]
        for t in range(1, tasks):
            alive = jnp.maximum(alive, keep_ref[t, b])
        flags.append(alive)

        @pl.when((alive > 0) & (live < kept))
        def _(live=live, b=b):
            chosen[live] = b

        live = live + alive
    for b in range(blocks):

        @pl.when((flags[b] == 0) & (live < kept))
        def _(live=live, b=b):
            chosen[live] = b

        live = live + (1 - flags[b])
    layer = layer_ref[0]
    per = kept // nf
    arrivals = []

    def fetch(source, target):
        copy = pltpu.make_async_copy(source, target, in_sems.at[len(arrivals)])
        arrivals.append(copy)
        copy.start()

    order = [(p + 1) % nf for p in range(nf)]
    for p in order:
        dest = lax.bitwise_xor(layer, p)
        for i in range(per):
            block = pl.ds(pl.multiple_of(chosen[dest * per + i] * width, width), width)
            for half, source in enumerate((gate, up)):
                fetch(source.at[:, block], stage.at[p, :, pl.ds((half * per + i) * width, width)])
    for slot in range(kept):
        block = pl.ds(pl.multiple_of(chosen[slot] * width, width), width)
        fetch(down.at[block, :], down_stage.at[pl.ds(slot * width, width), :])
    for slot in range(kept):
        for t in range(tasks):
            keep_out[t, slot] = keep_ref[t, chosen[slot]]
    leaving = []
    for place, p in enumerate(order):
        for copy in arrivals[place * 2 * per : (place + 1) * 2 * per]:
            copy.wait()
        leaving.append(pltpu.make_async_copy(stage.at[p], sends[p], out_sems.at[p]))
        leaving[-1].start()
    for copy in arrivals[2 * kept :]:
        copy.wait()
    leaving.append(pltpu.make_async_copy(down_stage, down_out, out_sems.at[nf]))
    leaving[-1].start()
    for copy in leaving:
        copy.wait()


def pick(nf, f, keep_mask, gate_weight, up_weight, down_weight):
    tasks, blocks = keep_mask.shape
    deep, local_width = gate_weight.shape
    width = local_width // blocks
    kept = blocks * 4 // 7
    hidden = kept * width
    q = hidden // nf
    if kept % nf == 0:
        out = pl.pallas_call(
            functools.partial(pick_kernel, nf, kept, width),
            in_specs=[pl.BlockSpec(memory_space=pltpu.SMEM)] * 2 + [pl.BlockSpec(memory_space=pl.ANY)] * 3,
            out_specs=[pl.BlockSpec(memory_space=pl.ANY)] * (nf + 1) + [pl.BlockSpec(memory_space=pltpu.SMEM)],
            out_shape=[jax.ShapeDtypeStruct((deep, 2 * q), BF16)] * nf
            + [jax.ShapeDtypeStruct((hidden, down_weight.shape[1]), BF16), jax.ShapeDtypeStruct((tasks, kept), jnp.int32)],
            scratch_shapes=[
                pltpu.SMEM((kept,), jnp.int32),
                pltpu.VMEM((nf, deep, 2 * q), BF16),
                pltpu.VMEM((hidden, down_weight.shape[1]), BF16),
                pltpu.SemaphoreType.DMA((3 * kept,)),
                pltpu.SemaphoreType.DMA((nf + 1,)),
            ],
            compiler_params=pltpu.CompilerParams(vmem_limit_bytes=32 * 2**20),
        )(f.reshape(1), keep_mask, gate_weight, up_weight, down_weight)
        return out[:nf], out[nf], out[nf + 1]
    alive = jnp.max(keep_mask, axis=0)
    chosen = jnp.argsort((1 - alive) * blocks + jnp.arange(blocks, dtype=jnp.int32))[:kept]
    gate_pick, up_pick = (
        jnp.take(w.reshape(deep, blocks, width), chosen, axis=1).reshape(deep, hidden) for w in (gate_weight, up_weight)
    )
    down_pick = jnp.take(down_weight.reshape(blocks, width, -1), chosen, axis=0).reshape(hidden, -1)
    sends = [
        jnp.concatenate([lax.dynamic_slice_in_dim(w, (f ^ p) * q, q, 1) for w in (gate_pick, up_pick)], axis=1)
        for p in range(nf)
    ]
    return sends, down_pick, jnp.take(keep_mask, chosen, axis=1)


def from_layers(pieces, f):
    n = len(pieces)
    stacked = jnp.zeros((n, *pieces[0].shape), pieces[0].dtype)
    for p, piece in enumerate(pieces):
        if p:
            piece = lax.ppermute(piece, "fsdp", [(i, i ^ p) for i in range(n)])
        stacked = lax.dynamic_update_index_in_dim(stacked, piece, f ^ p, 0)
    return stacked


def line_scatter(unit, n, axis, me):
    up = down = None
    for k in range(1, n):
        ahead, behind = unit(jnp.clip(me + n - k, 0, n - 1)), unit(jnp.clip(me - n + k, 0, n - 1))
        if k > 1:
            ahead, behind = ahead + up.astype(F32), behind + down.astype(F32)
        up = lax.ppermute(ahead.astype(BF16), axis, [(i, i + 1) for i in range(k)])
        down = lax.ppermute(behind.astype(BF16), axis, [(i, i - 1) for i in range(n - k, n)])
    return unit(me) + up.astype(F32) + down.astype(F32)


def layer_scatter(rows_of, weight, n, chip, order):
    held = list(range(n))
    got = {d: [] for d in held}
    for bit in order:
        sent = [d for d in held if d >> bit & 1]
        held = [d for d in held if not d >> bit & 1]
        part = dot_t(jnp.concatenate([rows_of(chip ^ d) for d in sent]), weight)
        for piece in zip(*(got[d] for d in sent)):
            part = part + jnp.concatenate(piece).astype(F32)
        arrived = lax.ppermute(part.astype(BF16), "seq", [(i, i ^ (2 << bit)) for i in range(2 * n)])
        for d, piece in zip(sent, jnp.split(arrived, len(sent))):
            got[d ^ (1 << bit)].append(piece)
    total = dot_t(rows_of(chip), weight)
    for piece in got[0]:
        total = total + piece.astype(F32)
    return total


def local(nf, ns, tokens, grad_out, gate_weight, up_weight, down_weight, keep_mask, task_ids):
    f, s = lax.axis_index("fsdp"), lax.axis_index("seq")
    core, chip, chips = s & 1, s >> 1, ns // 2
    rows, wide = tokens.shape
    deep = wide // nf
    every = nf * ns * rows
    swap = [(i, i ^ 1) for i in range(ns)]

    with jax.named_scope("grad_rows"):
        ids = from_layers([task_ids.reshape(ns, rows)] * nf, f)
        grads = from_layers([lax.dynamic_slice_in_dim(grad_out, (f ^ p) * deep, deep, 1) for p in range(nf)], f)
    with jax.named_scope("pick"):
        sends, down_pick, keep_pick = pick(nf, f, keep_mask, gate_weight, up_weight, down_weight)
    hidden_width = down_pick.shape[0]
    q = hidden_width // nf

    with jax.named_scope("weights"):
        weight = from_layers(sends, f).reshape(wide, 2 * q)

    half = wide // 2
    with jax.named_scope("token_rows"):
        own_rows = lax.dynamic_slice_in_dim(tokens, core * half, half, 1)
        twin_rows = lax.ppermute(lax.dynamic_slice_in_dim(tokens, (1 - core) * half, half, 1), "seq", swap)
        token_rows = jnp.where(core == 0, jnp.stack([own_rows, twin_rows]), jnp.stack([twin_rows, own_rows]))
        token_rows = lax.all_gather(token_rows, "fsdp", axis=1, tiled=False)
        grads = lax.all_gather(grads.reshape(nf * rows, deep), "seq", axis=0, tiled=True)
        token_rows, grads = lax.optimization_barrier((token_rows, grads))
        same_core = [[i for i in range(ns) if i & 1 == c] for c in range(2)]
        token_rows = lax.all_gather(
            token_rows.reshape(2 * nf * rows, half), "seq", axis=0, tiled=True, axis_index_groups=same_core
        )

    with jax.named_scope("hidden_grad"):
        hidden_grad = line_scatter(
            lambda j: dot_t(grads, lax.dynamic_slice_in_dim(down_pick, j * q, q, 0)), nf, "fsdp", f
        )

    with jax.named_scope("twin_weights"):
        mine = lax.dynamic_slice_in_dim(weight, core * half, half, 0)
        other = lax.ppermute(lax.dynamic_slice_in_dim(weight, (1 - core) * half, half, 0), "seq", swap)
        both_weight = jnp.concatenate([mine, other], axis=1)

    with jax.named_scope("mask"):
        ids = ids.transpose(1, 0, 2).reshape(every)
        tasks, kept = keep_pick.shape
        onehot = (ids[:, None] == jnp.arange(tasks, dtype=jnp.int32)[None, :]).astype(BF16)
        keep_columns = jnp.repeat(keep_pick.astype(BF16), hidden_width // kept, axis=1)
        mask = dot(onehot, lax.dynamic_slice_in_dim(keep_columns, f * q, q, 1))

    with jax.named_scope("elementwise"):
        pre = dot(token_rows, both_weight)
        pre = pre[:, : 2 * q] + lax.ppermute(pre[:, 2 * q :].astype(BF16), "seq", swap).astype(F32)
        gate_pre, up_pre = pre[:, :q], pre[:, q:]
        logistic = jax.nn.sigmoid(gate_pre)
        activated = gate_pre * logistic
        hidden = (activated * up_pre * mask).astype(BF16)
        masked_grad = hidden_grad * mask
        gate_grad = (masked_grad * up_pre * logistic * (1.0 + gate_pre * (1.0 - logistic))).astype(BF16)
        up_grad = (masked_grad * activated).astype(BF16)

    with jax.named_scope("layer_out"):
        hidden_all = lax.all_gather(hidden, "fsdp", axis=1, tiled=True)
        out_part = dot(hidden_all, down_pick).astype(BF16)
        out = lax.psum_scatter(out_part, "seq", scatter_dimension=0, tiled=True)
        out = lax.all_to_all(out.reshape(nf, rows, deep), "fsdp", 0, 0, tiled=False)
        layer_out = out.transpose(1, 0, 2).reshape(rows, wide)

    with jax.named_scope("input_grad"):
        own = jnp.concatenate([gate_grad, up_grad], axis=1)
        both = jnp.concatenate([own, lax.ppermute(own, "seq", swap)], axis=1).reshape(chips, every // chips, 4 * q)
        rows_of = lambda c: lax.dynamic_index_in_dim(both, c, 0, keepdims=False)
        bits = list(range(chips.bit_length() - 1))
        first = layer_scatter(rows_of, both_weight[: half // 2], chips, chip, bits)
        second = layer_scatter(rows_of, both_weight[half // 2 :], chips, chip, bits[::-1])
        part = jnp.concatenate([first, second], axis=1).reshape(2, nf, rows, half)
        total = line_scatter(
            lambda j: lax.dynamic_index_in_dim(part, j, 1, keepdims=False), nf, "fsdp", f
        ).astype(BF16)
        here = lax.dynamic_index_in_dim(total, core, 0, keepdims=False)
        there = lax.ppermute(lax.dynamic_index_in_dim(total, 1 - core, 0, keepdims=False), "seq", swap)
        input_grad = jnp.where(
            core == 0, jnp.concatenate([here, there], axis=1), jnp.concatenate([there, here], axis=1)
        )
    return layer_out, input_grad


def solution(mesh):
    placed = (
        P(("fsdp", "seq"), None),
        P(("fsdp", "seq"), None),
        P("fsdp", "seq"),
        P("fsdp", "seq"),
        P("seq", "fsdp"),
        P(None, "seq"),
        P("fsdp"),
    )
    return jax.shard_map(
        functools.partial(local, mesh.shape["fsdp"], mesh.shape["seq"]),
        mesh=mesh,
        in_specs=placed,
        out_specs=(P(("fsdp", "seq"), None), P(("fsdp", "seq"), None)),
        check_vma=False,
    )
```

```python
import functools

import jax
import jax.numpy as jnp
from jax import lax
from jax.experimental import pallas as pl
from jax.experimental.pallas import tpu as pltpu
from jax.sharding import PartitionSpec as P

BF16, F32 = jnp.bfloat16, jnp.float32


def dot_t(left, right):
    return lax.dot_general(left, right, (((1,), (1,)), ((), ())), preferred_element_type=F32)


def dot(left, right):
    return jnp.dot(left, right, preferred_element_type=F32)


def forward(gate_pre, up_pre, mask):
    logistic = 1.0 / (1.0 + jnp.exp(-gate_pre))
    activated = gate_pre * logistic * mask
    return activated * up_pre, mask * up_pre * logistic * (1.0 + gate_pre * (1.0 - logistic)), activated


def factor_kernel(own_ref, twin_ref, mask_ref, factor_ref):
    q = mask_ref.shape[1]
    gate_pre, up_pre = (own_ref[:, i * q : (i + 1) * q] + twin_ref[:, i * q : (i + 1) * q].astype(F32) for i in range(2))
    _, factor_ref[:, :q], factor_ref[:, q:] = forward(gate_pre, up_pre, mask_ref[...])


def factors(own, twin, mask):
    rows, wide = own.shape
    q = wide // 2
    if q % 128:
        pre = own + twin.astype(F32)
        return jnp.concatenate(forward(pre[:, :q], pre[:, q:], mask)[1:], axis=1)
    tile = rows // 4
    block = lambda columns: pl.BlockSpec((tile, columns), lambda i: (i, 0))
    return pl.pallas_call(
        factor_kernel,
        grid=(4,),
        in_specs=[block(wide), block(wide), block(q)],
        out_specs=block(wide),
        out_shape=jax.ShapeDtypeStruct((rows, wide), F32),
        compiler_params=pltpu.CompilerParams(vmem_limit_bytes=32 * 2**20),
        cost_estimate=pl.CostEstimate(flops=0, bytes_accessed=300 * 2**20, transcendentals=0),
    )(own, twin, mask)


def pick_kernel(nf, kept, width, layer_ref, keep_ref, gate, up, down, *rest):
    sends, (down_out, keep_out) = rest[:nf], rest[nf : nf + 2]
    chosen, stage, down_stage, in_sems, out_sems = rest[nf + 2 :]
    tasks, blocks = keep_ref.shape
    for slot in range(kept):
        chosen[slot] = 0
    live = jnp.int32(0)
    flags = []
    for b in range(blocks):
        alive = keep_ref[0, b]
        for t in range(1, tasks):
            alive = jnp.maximum(alive, keep_ref[t, b])
        flags.append(alive)

        @pl.when((alive > 0) & (live < kept))
        def _(live=live, b=b):
            chosen[live] = b

        live = live + alive
    for b in range(blocks):

        @pl.when((flags[b] == 0) & (live < kept))
        def _(live=live, b=b):
            chosen[live] = b

        live = live + (1 - flags[b])
    layer = layer_ref[0]
    per = kept // nf
    arrivals = []

    def fetch(source, target):
        copy = pltpu.make_async_copy(source, target, in_sems.at[len(arrivals)])
        arrivals.append(copy)
        copy.start()

    order = [(p + 1) % nf for p in range(nf)]
    for p in order:
        dest = lax.bitwise_xor(layer, p)
        for i in range(per):
            block = pl.ds(pl.multiple_of(chosen[dest * per + i] * width, width), width)
            for half, source in enumerate((gate, up)):
                fetch(source.at[:, block], stage.at[p, :, pl.ds((half * per + i) * width, width)])
    for slot in range(kept):
        block = pl.ds(pl.multiple_of(chosen[slot] * width, width), width)
        fetch(down.at[block, :], down_stage.at[pl.ds(slot * width, width), :])
    for slot in range(kept):
        for t in range(tasks):
            keep_out[t, slot] = keep_ref[t, chosen[slot]]
    leaving = []
    for place, p in enumerate(order):
        for copy in arrivals[place * 2 * per : (place + 1) * 2 * per]:
            copy.wait()
        leaving.append(pltpu.make_async_copy(stage.at[p], sends[p], out_sems.at[p]))
        leaving[-1].start()
    for copy in arrivals[2 * kept :]:
        copy.wait()
    leaving.append(pltpu.make_async_copy(down_stage, down_out, out_sems.at[nf]))
    leaving[-1].start()
    for copy in leaving:
        copy.wait()


def pick(nf, f, keep_mask, gate_weight, up_weight, down_weight):
    tasks, blocks = keep_mask.shape
    deep, local_width = gate_weight.shape
    width = local_width // blocks
    kept = blocks * 4 // 7
    hidden = kept * width
    q = hidden // nf
    if kept % nf == 0:
        out = pl.pallas_call(
            functools.partial(pick_kernel, nf, kept, width),
            in_specs=[pl.BlockSpec(memory_space=pltpu.SMEM)] * 2 + [pl.BlockSpec(memory_space=pl.ANY)] * 3,
            out_specs=[pl.BlockSpec(memory_space=pl.ANY)] * (nf + 1) + [pl.BlockSpec(memory_space=pltpu.SMEM)],
            out_shape=[jax.ShapeDtypeStruct((deep, 2 * q), BF16)] * nf
            + [jax.ShapeDtypeStruct((hidden, down_weight.shape[1]), BF16), jax.ShapeDtypeStruct((tasks, kept), jnp.int32)],
            scratch_shapes=[
                pltpu.SMEM((kept,), jnp.int32),
                pltpu.VMEM((nf, deep, 2 * q), BF16),
                pltpu.VMEM((hidden, down_weight.shape[1]), BF16),
                pltpu.SemaphoreType.DMA((3 * kept,)),
                pltpu.SemaphoreType.DMA((nf + 1,)),
            ],
            compiler_params=pltpu.CompilerParams(vmem_limit_bytes=56 * 2**20),
            cost_estimate=pl.CostEstimate(flops=0, bytes_accessed=12 * deep * hidden, transcendentals=0),
        )(f.reshape(1), keep_mask, gate_weight, up_weight, down_weight)
        return out[:nf], out[nf], out[nf + 1]
    alive = jnp.max(keep_mask, axis=0)
    chosen = jnp.argsort((1 - alive) * blocks + jnp.arange(blocks, dtype=jnp.int32))[:kept]
    gate_pick, up_pick = (
        jnp.take(w.reshape(deep, blocks, width), chosen, axis=1).reshape(deep, hidden) for w in (gate_weight, up_weight)
    )
    down_pick = jnp.take(down_weight.reshape(blocks, width, -1), chosen, axis=0).reshape(hidden, -1)
    sends = [
        jnp.concatenate([lax.dynamic_slice_in_dim(w, (f ^ p) * q, q, 1) for w in (gate_pick, up_pick)], axis=1)
        for p in range(nf)
    ]
    return sends, down_pick, jnp.take(keep_mask, chosen, axis=1)


after = lax.optimization_barrier


def across(piece, p, n):
    return lax.ppermute(piece, "fsdp", [(i, i ^ p) for i in range(n)]) if p else piece


def in_order(pieces, f):
    stacked = jnp.zeros((len(pieces), *pieces[0].shape), pieces[0].dtype)
    for p, piece in enumerate(pieces):
        stacked = lax.dynamic_update_index_in_dim(stacked, piece, f ^ p, 0)
    return stacked


def line_steps(unit, n, axis, me):
    up = down = None
    for k in range(1, n):
        ahead, behind = unit(jnp.clip(me + n - k, 0, n - 1)), unit(jnp.clip(me - n + k, 0, n - 1))
        if k > 1:
            ahead, behind = ahead + up.astype(F32), behind + down.astype(F32)
        up = lax.ppermute(ahead.astype(BF16), axis, [(i, i + 1) for i in range(k)])
        down = lax.ppermute(behind.astype(BF16), axis, [(i, i - 1) for i in range(n - k, n)])
        up, down = yield up, down
    return unit(me) + up.astype(F32) + down.astype(F32)


def layers_sum(unit, n, me):
    arrived = [across(unit(me ^ p).astype(BF16), p, n) for p in range(1, n)]
    arrived = yield arrived
    total = unit(me)
    for piece in arrived:
        total = total + piece.astype(F32)
    return total


def finish(steps, arrived):
    try:
        while True:
            arrived = steps.send(arrived)
    except StopIteration as end:
        return end.value


def assemble_kernel(places, *refs):
    out = refs[-1]
    for row, column, part, first, count in places:
        width = refs[part].shape[1]
        out[pl.ds(row, count), pl.ds(column, width)] = refs[part][pl.ds(first, count), :]


def assemble(arrays, places, shape):
    if shape[0] * shape[1] > 2**23:
        return jnp.concatenate(arrays)
    return pl.pallas_call(
        functools.partial(assemble_kernel, places),
        in_specs=[pl.BlockSpec(memory_space=pltpu.VMEM)] * len(arrays),
        out_specs=pl.BlockSpec(memory_space=pltpu.VMEM),
        out_shape=jax.ShapeDtypeStruct(shape, BF16),
        compiler_params=pltpu.CompilerParams(vmem_limit_bytes=32 * 2**20),
    )(*arrays)


def stack_rows(arrays):
    rows, columns = arrays[0].shape
    return assemble(arrays, [(d * rows, 0, d, 0, rows) for d in range(len(arrays))], (len(arrays) * rows, columns))


def seq_gather(x, n):
    return [x] + [lax.ppermute(x, "seq", [(i, i ^ d) for i in range(n)]) for d in range(1, n)]


def layer_scatter(rows, weight, n):
    pieces = jnp.split(rows, n)
    count = n.bit_length() - 1
    halves = jnp.split(weight, 2)
    held = [list(range(n)) for _ in halves]
    got = [{d: [] for d in range(n)} for _ in halves]
    for step in range(count):
        for side, bit in enumerate((step, count - 1 - step)):
            sent = [d for d in held[side] if d >> bit & 1]
            held[side] = [d for d in held[side] if not d >> bit & 1]
            part = dot_t(jnp.concatenate([pieces[d] for d in sent]), halves[side])
            for piece in zip(*(got[side][d] for d in sent)):
                part = part + jnp.concatenate(piece).astype(F32)
            arrived = lax.ppermute(part.astype(BF16), "seq", [(i, i ^ (2 << bit)) for i in range(2 * n)])
            for d, piece in zip(sent, jnp.split(arrived, len(sent))):
                got[side][d ^ (1 << bit)].append(piece)
        got = yield got
    totals = []
    for side, half in enumerate(halves):
        total = dot_t(pieces[0], half)
        for piece in got[side][0]:
            total = total + piece.astype(F32)
        totals.append(total)
    return jnp.concatenate(totals, axis=1)


def local(nf, ns, tokens, grad_out, gate_weight, up_weight, down_weight, keep_mask, task_ids):
    f, s = lax.axis_index("fsdp"), lax.axis_index("seq")
    core, chip, chips = s & 1, s >> 1, ns // 2
    rows, wide = tokens.shape
    deep, half = wide // nf, wide // 2
    every = nf * ns * rows
    swap = [(i, i ^ 1) for i in range(ns)]

    with jax.named_scope("pick"):
        sends, down_pick, keep_pick = pick(nf, f, keep_mask, gate_weight, up_weight, down_weight)
    hidden_width = down_pick.shape[0]
    q = hidden_width // nf

    with jax.named_scope("grad_rows"):
        extra = jnp.zeros((8 * deep,), BF16).at[: ns * rows].set(task_ids.astype(BF16)).reshape(8, deep)
        pieces = [
            jnp.concatenate([lax.dynamic_slice_in_dim(grad_out, (f ^ p) * deep, deep, 1), extra]) for p in range(nf)
        ]
        grads = in_order([across(piece, p, nf) for p, piece in enumerate(pieces)], f)
        ids = grads[:, rows:].reshape(nf, 8 * deep)[:, : ns * rows].reshape(nf, chips, 2 * rows)
        ids = ids.transpose(1, 0, 2).reshape(every)
        grads, sends = after((grads[:, :rows].reshape(nf * rows, deep), sends))
        got = [sends[0], *(across(sends[p], p, nf) for p in (1, 2))]
        grads = seq_gather(grads, ns)

    with jax.named_scope("token_rows"):
        own_rows = lax.dynamic_slice_in_dim(tokens, core * half, half, 1)
        twin_rows = lax.ppermute(lax.dynamic_slice_in_dim(tokens, (1 - core) * half, half, 1), "seq", swap)
        token_rows = jnp.where(
            core == 0, jnp.concatenate([own_rows, twin_rows]), jnp.concatenate([twin_rows, own_rows])
        )
        token_rows = lax.all_gather(token_rows, "fsdp", axis=0, tiled=True)
        token_rows, grads, got, sends = after((token_rows, grads, got, sends))
        same_core = [[i for i in range(ns) if i & 1 == c] for c in range(2)]
        token_rows = lax.all_gather(token_rows, "seq", axis=0, tiled=True, axis_index_groups=same_core)

    with jax.named_scope("hidden_grad"):
        got += [across(sends[p], p, nf) for p in range(3, nf)]
        part = dot_t(stack_rows(grads[::2] + grads[1::2]), down_pick)
        steps = line_steps(lambda j: lax.dynamic_slice_in_dim(part, j * q, q, 1), nf, "fsdp", f)
        arrived, got = after((next(steps), got))

    with jax.named_scope("weights"):
        weight = in_order(got, f).reshape(wide, 2 * q)
        mine = lax.dynamic_slice_in_dim(weight, core * half, half, 0)
        other = lax.ppermute(lax.dynamic_slice_in_dim(weight, (1 - core) * half, half, 0), "seq", swap)
        both_weight = jnp.concatenate([mine, other], axis=1)

    with jax.named_scope("mask"):
        tasks, kept = keep_pick.shape
        onehot = (ids[:, None] == jnp.arange(tasks, dtype=jnp.int32)[None, :]).astype(BF16)
        keep_columns = jnp.repeat(keep_pick.astype(BF16), hidden_width // kept, axis=1)
        mask = dot(onehot, lax.dynamic_slice_in_dim(keep_columns, f * q, q, 1))

    with jax.named_scope("forward"):
        pre = dot(token_rows, both_weight)
        arrived, pre = after((steps.send(arrived), pre))
        own, twin = pre[:, : 2 * q], lax.ppermute(pre[:, 2 * q :].astype(BF16), "seq", swap)
        pre = own + twin.astype(F32)
        hidden = forward(pre[:, :q], pre[:, q:], mask)[0]
        hidden = hidden.astype(BF16).reshape(chips, nf, 2, rows, q).transpose(0, 2, 1, 3, 4).reshape(every, q)
        hidden, own = after((hidden, own))
        hidden_all = lax.all_gather(hidden, "fsdp", axis=1, tiled=True)
        factor = factors(own, twin, mask)
        if nf > 3:
            arrived = steps.send(arrived)
        factor = factor.reshape(chips, nf, 2, rows, 2 * q)
        factor = jnp.stack([lax.dynamic_index_in_dim(factor, chip ^ d, 0, keepdims=False) for d in range(chips)])
        arrived, factor = after((arrived, factor))
        hidden_grad = finish(steps, arrived)

    with jax.named_scope("input_grad"):
        hidden_grad = hidden_grad.reshape(2, every // 2, q)
        own = []
        for c in range(2):
            chunk = lax.dynamic_index_in_dim(hidden_grad, c ^ core, 0, keepdims=False)
            scale = factor[:, :, c].reshape(every // 2, 2 * q)
            own.append((scale * jnp.concatenate([chunk, chunk], axis=1)).astype(BF16))
        both = [jnp.concatenate([own[c], lax.ppermute(own[c], "seq", swap)], axis=1) for c in range(2)]

        def over_layers(part):
            part = part.reshape(nf, rows, half)
            return layers_sum(lambda j: lax.dynamic_index_in_dim(part, j, 0, keepdims=False), nf, f)

        steps = chips.bit_length() - 1
        first = layer_scatter(both[0], both_weight, chips)
        arrived = next(first)
        for _ in range(steps - 1):
            arrived = first.send(arrived)
        arrived, both[1] = after((arrived, both[1]))
        second = layer_scatter(both[1], both_weight, chips)
        waiting, hidden_all = after((next(second), hidden_all))
        for _ in range(steps - 1):
            waiting = second.send(waiting)
        first = over_layers(finish(first, arrived))
        arrived, waiting = after((next(first), waiting))
        second = over_layers(finish(second, waiting))
        totals = [finish(first, arrived).astype(BF16), finish(second, next(second)).astype(BF16)]
        here = jnp.where(core == 0, totals[0], totals[1])
        there = lax.ppermute(jnp.where(core == 0, totals[1], totals[0]), "seq", swap)
        input_grad = jnp.where(
            core == 0, jnp.concatenate([here, there], axis=1), jnp.concatenate([there, here], axis=1)
        )

    with jax.named_scope("layer_out"):
        out_part = dot(hidden_all, down_pick).astype(BF16)
        out = lax.psum_scatter(out_part, "seq", scatter_dimension=0, tiled=True)
        out = lax.all_to_all(out.reshape(nf, rows, deep), "fsdp", 0, 0, tiled=False)
        layer_out = out.transpose(1, 0, 2).reshape(rows, wide)
    return layer_out, input_grad


def solution(mesh):
    placed = (
        P(("fsdp", "seq"), None),
        P(("fsdp", "seq"), None),
        P("fsdp", "seq"),
        P("fsdp", "seq"),
        P("seq", "fsdp"),
        P(None, "seq"),
        P("fsdp"),
    )
    return jax.shard_map(
        functools.partial(local, mesh.shape["fsdp"], mesh.shape["seq"]),
        mesh=mesh,
        in_specs=placed,
        out_specs=(P(("fsdp", "seq"), None), P(("fsdp", "seq"), None)),
        check_vma=False,
    )
```

```python
import functools

import jax
import jax.numpy as jnp
from jax import lax
from jax.experimental import pallas as pl
from jax.experimental.pallas import tpu as pltpu
from jax.sharding import PartitionSpec as P

BF16, F32 = jnp.bfloat16, jnp.float32


def dot_t(left, right):
    return lax.dot_general(left, right, (((1,), (1,)), ((), ())), preferred_element_type=F32)


def dot(left, right):
    return jnp.dot(left, right, preferred_element_type=F32)


def forward(gate_pre, up_pre, mask):
    logistic = 1.0 / (1.0 + jnp.exp(-gate_pre))
    activated = gate_pre * logistic * mask
    return activated * up_pre, mask * up_pre * logistic * (1.0 + gate_pre * (1.0 - logistic)), activated


def factor_kernel(own_ref, twin_ref, mask_ref, factor_ref):
    q = mask_ref.shape[1]
    gate_pre, up_pre = (own_ref[:, i * q : (i + 1) * q] + twin_ref[:, i * q : (i + 1) * q].astype(F32) for i in range(2))
    _, factor_ref[:, :q], factor_ref[:, q:] = forward(gate_pre, up_pre, mask_ref[...])


def factors(own, twin, mask):
    rows, wide = own.shape
    q = wide // 2
    if q % 128:
        pre = own + twin.astype(F32)
        return jnp.concatenate(forward(pre[:, :q], pre[:, q:], mask)[1:], axis=1)
    tile = rows // 4
    block = lambda columns: pl.BlockSpec((tile, columns), lambda i: (i, 0))
    return pl.pallas_call(
        factor_kernel,
        grid=(4,),
        in_specs=[block(wide), block(wide), block(q)],
        out_specs=block(wide),
        out_shape=jax.ShapeDtypeStruct((rows, wide), F32),
        compiler_params=pltpu.CompilerParams(vmem_limit_bytes=32 * 2**20),
        cost_estimate=pl.CostEstimate(flops=0, bytes_accessed=300 * 2**20, transcendentals=0),
    )(own, twin, mask)


def pick_kernel(nf, kept, width, layer_ref, keep_ref, gate, up, down, *rest):
    sends, (down_out, keep_out) = rest[:nf], rest[nf : nf + 2]
    chosen, stage, down_stage, in_sems, out_sems = rest[nf + 2 :]
    tasks, blocks = keep_ref.shape
    for slot in range(kept):
        chosen[slot] = 0
    live = jnp.int32(0)
    flags = []
    for b in range(blocks):
        alive = keep_ref[0, b]
        for t in range(1, tasks):
            alive = jnp.maximum(alive, keep_ref[t, b])
        flags.append(alive)

        @pl.when((alive > 0) & (live < kept))
        def _(live=live, b=b):
            chosen[live] = b

        live = live + alive
    for b in range(blocks):

        @pl.when((flags[b] == 0) & (live < kept))
        def _(live=live, b=b):
            chosen[live] = b

        live = live + (1 - flags[b])
    layer = layer_ref[0]
    per = kept // nf
    arrivals = []

    def fetch(source, target):
        copy = pltpu.make_async_copy(source, target, in_sems.at[len(arrivals)])
        arrivals.append(copy)
        copy.start()

    order = [(p + 1) % nf for p in range(nf)]
    for p in order:
        dest = lax.bitwise_xor(layer, p)
        for i in range(per):
            block = pl.ds(pl.multiple_of(chosen[dest * per + i] * width, width), width)
            for half, source in enumerate((gate, up)):
                fetch(source.at[:, block], stage.at[p, :, pl.ds((half * per + i) * width, width)])
    for slot in range(kept):
        block = pl.ds(pl.multiple_of(chosen[slot] * width, width), width)
        fetch(down.at[block, :], down_stage.at[pl.ds(slot * width, width), :])
    for slot in range(kept):
        for t in range(tasks):
            keep_out[t, slot] = keep_ref[t, chosen[slot]]
    leaving = []
    for place, p in enumerate(order):
        for copy in arrivals[place * 2 * per : (place + 1) * 2 * per]:
            copy.wait()
        leaving.append(pltpu.make_async_copy(stage.at[p], sends[p], out_sems.at[p]))
        leaving[-1].start()
    for copy in arrivals[2 * kept :]:
        copy.wait()
    leaving.append(pltpu.make_async_copy(down_stage, down_out, out_sems.at[nf]))
    leaving[-1].start()
    for copy in leaving:
        copy.wait()


def pick(nf, f, keep_mask, gate_weight, up_weight, down_weight):
    tasks, blocks = keep_mask.shape
    deep, local_width = gate_weight.shape
    width = local_width // blocks
    kept = blocks * 4 // 7
    hidden = kept * width
    q = hidden // nf
    if kept % nf == 0:
        out = pl.pallas_call(
            functools.partial(pick_kernel, nf, kept, width),
            in_specs=[pl.BlockSpec(memory_space=pltpu.SMEM)] * 2 + [pl.BlockSpec(memory_space=pl.ANY)] * 3,
            out_specs=[pl.BlockSpec(memory_space=pl.ANY)] * (nf + 1) + [pl.BlockSpec(memory_space=pltpu.SMEM)],
            out_shape=[jax.ShapeDtypeStruct((deep, 2 * q), BF16)] * nf
            + [jax.ShapeDtypeStruct((hidden, down_weight.shape[1]), BF16), jax.ShapeDtypeStruct((tasks, kept), jnp.int32)],
            scratch_shapes=[
                pltpu.SMEM((kept,), jnp.int32),
                pltpu.VMEM((nf, deep, 2 * q), BF16),
                pltpu.VMEM((hidden, down_weight.shape[1]), BF16),
                pltpu.SemaphoreType.DMA((3 * kept,)),
                pltpu.SemaphoreType.DMA((nf + 1,)),
            ],
            compiler_params=pltpu.CompilerParams(vmem_limit_bytes=56 * 2**20),
            cost_estimate=pl.CostEstimate(flops=0, bytes_accessed=12 * deep * hidden, transcendentals=0),
        )(f.reshape(1), keep_mask, gate_weight, up_weight, down_weight)
        return out[:nf], out[nf], out[nf + 1]
    alive = jnp.max(keep_mask, axis=0)
    chosen = jnp.argsort((1 - alive) * blocks + jnp.arange(blocks, dtype=jnp.int32))[:kept]
    gate_pick, up_pick = (
        jnp.take(w.reshape(deep, blocks, width), chosen, axis=1).reshape(deep, hidden) for w in (gate_weight, up_weight)
    )
    down_pick = jnp.take(down_weight.reshape(blocks, width, -1), chosen, axis=0).reshape(hidden, -1)
    sends = [
        jnp.concatenate([lax.dynamic_slice_in_dim(w, (f ^ p) * q, q, 1) for w in (gate_pick, up_pick)], axis=1)
        for p in range(nf)
    ]
    return sends, down_pick, jnp.take(keep_mask, chosen, axis=1)


after = lax.optimization_barrier


def across(piece, p, n):
    return lax.ppermute(piece, "fsdp", [(i, i ^ p) for i in range(n)]) if p else piece


def in_order(pieces, f):
    stacked = jnp.zeros((len(pieces), *pieces[0].shape), pieces[0].dtype)
    for p, piece in enumerate(pieces):
        stacked = lax.dynamic_update_index_in_dim(stacked, piece, f ^ p, 0)
    return stacked


def line_steps(unit, n, axis, me):
    up = down = None
    for k in range(1, n):
        ahead, behind = unit(jnp.clip(me + n - k, 0, n - 1)), unit(jnp.clip(me - n + k, 0, n - 1))
        if k > 1:
            ahead, behind = ahead + up.astype(F32), behind + down.astype(F32)
        up = lax.ppermute(ahead.astype(BF16), axis, [(i, i + 1) for i in range(k)])
        down = lax.ppermute(behind.astype(BF16), axis, [(i, i - 1) for i in range(n - k, n)])
        up, down = yield up, down
    return unit(me) + up.astype(F32) + down.astype(F32)


def layers_sum(unit, n, me):
    arrived = [across(unit(me ^ p).astype(BF16), p, n) for p in range(1, n)]
    arrived = yield arrived
    total = unit(me)
    for piece in arrived:
        total = total + piece.astype(F32)
    return total


def finish(steps, arrived):
    try:
        while True:
            arrived = steps.send(arrived)
    except StopIteration as end:
        return end.value


def assemble_kernel(places, *refs):
    out = refs[-1]
    for row, column, part, first, count in places:
        width = refs[part].shape[1]
        out[pl.ds(row, count), pl.ds(column, width)] = refs[part][pl.ds(first, count), :]


def assemble(arrays, places, shape):
    if shape[0] * shape[1] > 2**23:
        return jnp.concatenate(arrays)
    return pl.pallas_call(
        functools.partial(assemble_kernel, places),
        in_specs=[pl.BlockSpec(memory_space=pltpu.VMEM)] * len(arrays),
        out_specs=pl.BlockSpec(memory_space=pltpu.VMEM),
        out_shape=jax.ShapeDtypeStruct(shape, BF16),
        compiler_params=pltpu.CompilerParams(vmem_limit_bytes=32 * 2**20),
    )(*arrays)


def stack_rows(arrays):
    rows, columns = arrays[0].shape
    return assemble(arrays, [(d * rows, 0, d, 0, rows) for d in range(len(arrays))], (len(arrays) * rows, columns))


def seq_gather(x, n):
    return [x] + [lax.ppermute(x, "seq", [(i, i ^ d) for i in range(n)]) for d in range(1, n)]


def layer_scatter(rows, weight, n):
    pieces = jnp.split(rows, n)
    count = n.bit_length() - 1
    halves = jnp.split(weight, 2)
    held = [list(range(n)) for _ in halves]
    got = [{d: [] for d in range(n)} for _ in halves]
    for step in range(count):
        for side, bit in enumerate((step, count - 1 - step)):
            sent = [d for d in held[side] if d >> bit & 1]
            held[side] = [d for d in held[side] if not d >> bit & 1]
            part = dot_t(jnp.concatenate([pieces[d] for d in sent]), halves[side])
            for piece in zip(*(got[side][d] for d in sent)):
                part = part + jnp.concatenate(piece).astype(F32)
            arrived = lax.ppermute(part.astype(BF16), "seq", [(i, i ^ (2 << bit)) for i in range(2 * n)])
            for d, piece in zip(sent, jnp.split(arrived, len(sent))):
                got[side][d ^ (1 << bit)].append(piece)
        got = yield got
    totals = []
    for side, half in enumerate(halves):
        total = dot_t(pieces[0], half)
        for piece in got[side][0]:
            total = total + piece.astype(F32)
        totals.append(total)
    return jnp.concatenate(totals, axis=1)


def local(nf, ns, tokens, grad_out, gate_weight, up_weight, down_weight, keep_mask, task_ids):
    f, s = lax.axis_index("fsdp"), lax.axis_index("seq")
    core, chip, chips = s & 1, s >> 1, ns // 2
    rows, wide = tokens.shape
    deep, half = wide // nf, wide // 2
    every = nf * ns * rows
    swap = [(i, i ^ 1) for i in range(ns)]

    with jax.named_scope("pick"):
        sends, down_pick, keep_pick = pick(nf, f, keep_mask, gate_weight, up_weight, down_weight)
    hidden_width = down_pick.shape[0]
    q = hidden_width // nf

    with jax.named_scope("grad_rows"):
        extra = jnp.zeros((8 * deep,), BF16).at[: ns * rows].set(task_ids.astype(BF16)).reshape(8, deep)
        pieces = [
            jnp.concatenate([lax.dynamic_slice_in_dim(grad_out, (f ^ p) * deep, deep, 1), extra]) for p in range(nf)
        ]
        grads = in_order([across(piece, p, nf) for p, piece in enumerate(pieces)], f)
        ids = grads[:, rows:].reshape(nf, 8 * deep)[:, : ns * rows].reshape(nf, chips, 2 * rows)
        ids = ids.transpose(1, 0, 2).reshape(every)
        grads, sends = after((grads[:, :rows].reshape(nf * rows, deep), sends))
        got = [sends[0], *(across(sends[p], p, nf) for p in (1, 2))]
        grads = seq_gather(grads, ns)

    with jax.named_scope("token_rows"):
        own_rows = lax.dynamic_slice_in_dim(tokens, core * half, half, 1)
        twin_rows = lax.ppermute(lax.dynamic_slice_in_dim(tokens, (1 - core) * half, half, 1), "seq", swap)
        token_rows = jnp.where(
            core == 0, jnp.concatenate([own_rows, twin_rows]), jnp.concatenate([twin_rows, own_rows])
        )
        token_rows = lax.all_gather(token_rows, "fsdp", axis=0, tiled=True)
        token_rows, grads, got, sends = after((token_rows, grads, got, sends))
        same_core = [[i for i in range(ns) if i & 1 == c] for c in range(2)]
        token_rows = lax.all_gather(token_rows, "seq", axis=0, tiled=True, axis_index_groups=same_core)

    with jax.named_scope("hidden_grad"):
        got += [across(sends[p], p, nf) for p in range(3, nf)]
        part = dot_t(stack_rows(grads[::2] + grads[1::2]), down_pick).astype(BF16)
        steps = line_steps(lambda j: lax.dynamic_slice_in_dim(part, j * q, q, 1).astype(F32), nf, "fsdp", f)
        arrived, got = after((next(steps), got))

    with jax.named_scope("weights"):
        weight = in_order(got, f).reshape(wide, 2 * q)
        mine = lax.dynamic_slice_in_dim(weight, core * half, half, 0)
        other = lax.ppermute(lax.dynamic_slice_in_dim(weight, (1 - core) * half, half, 0), "seq", swap)
        both_weight = jnp.concatenate([mine, other], axis=1)

    with jax.named_scope("mask"):
        tasks, kept = keep_pick.shape
        onehot = (ids[:, None] == jnp.arange(tasks, dtype=jnp.int32)[None, :]).astype(BF16)
        keep_columns = jnp.repeat(keep_pick.astype(BF16), hidden_width // kept, axis=1)
        mask = dot(onehot, lax.dynamic_slice_in_dim(keep_columns, f * q, q, 1))

    with jax.named_scope("forward"):
        pre = dot(token_rows, both_weight)
        arrived, pre = after((steps.send(arrived), pre))
        own, twin = pre[:, : 2 * q], lax.ppermute(pre[:, 2 * q :].astype(BF16), "seq", swap)
        pre = own + twin.astype(F32)
        hidden = forward(pre[:, :q], pre[:, q:], mask)[0]
        hidden = hidden.astype(BF16).reshape(chips, nf, 2, rows, q).transpose(0, 2, 1, 3, 4).reshape(every, q)
        hidden, own = after((hidden, own))
        hidden_all = lax.all_gather(hidden, "fsdp", axis=1, tiled=True)
        factor = factors(own, twin, mask)
        if nf > 3:
            arrived = steps.send(arrived)
        factor = factor.reshape(chips, nf, 2, rows, 2 * q)
        factor = jnp.stack([lax.dynamic_index_in_dim(factor, chip ^ d, 0, keepdims=False) for d in range(chips)])
        arrived, factor = after((arrived, factor))
        hidden_grad = finish(steps, arrived)

    with jax.named_scope("input_grad"):
        hidden_grad = hidden_grad.reshape(2, every // 2, q)
        own = []
        for c in range(2):
            chunk = lax.dynamic_index_in_dim(hidden_grad, c ^ core, 0, keepdims=False)
            scale = factor[:, :, c].reshape(every // 2, 2 * q)
            own.append((scale * jnp.concatenate([chunk, chunk], axis=1)).astype(BF16))
        both = [jnp.concatenate([own[c], lax.ppermute(own[c], "seq", swap)], axis=1) for c in range(2)]

        def over_layers(part):
            part = part.reshape(nf, rows, half)
            return layers_sum(lambda j: lax.dynamic_index_in_dim(part, j, 0, keepdims=False), nf, f)

        steps = chips.bit_length() - 1
        first = layer_scatter(both[0], both_weight, chips)
        arrived = next(first)
        for _ in range(steps - 1):
            arrived = first.send(arrived)
        arrived, both[1] = after((arrived, both[1]))
        second = layer_scatter(both[1], both_weight, chips)
        waiting, hidden_all = after((next(second), hidden_all))
        for _ in range(steps - 1):
            waiting = second.send(waiting)
        first = over_layers(finish(first, arrived))
        arrived, waiting = after((next(first), waiting))
        second = over_layers(finish(second, waiting))
        totals = [finish(first, arrived).astype(BF16), finish(second, next(second)).astype(BF16)]
        here = jnp.where(core == 0, totals[0], totals[1])
        there = lax.ppermute(jnp.where(core == 0, totals[1], totals[0]), "seq", swap)
        input_grad = jnp.where(
            core == 0, jnp.concatenate([here, there], axis=1), jnp.concatenate([there, here], axis=1)
        )

    with jax.named_scope("layer_out"):
        out_part = dot(hidden_all, down_pick).astype(BF16)
        out = lax.psum_scatter(out_part, "seq", scatter_dimension=0, tiled=True)
        out = lax.all_to_all(out.reshape(nf, rows, deep), "fsdp", 0, 0, tiled=False)
        layer_out = out.transpose(1, 0, 2).reshape(rows, wide)
    return layer_out, input_grad


def solution(mesh):
    placed = (
        P(("fsdp", "seq"), None),
        P(("fsdp", "seq"), None),
        P("fsdp", "seq"),
        P("fsdp", "seq"),
        P("seq", "fsdp"),
        P(None, "seq"),
        P("fsdp"),
    )
    return jax.shard_map(
        functools.partial(local, mesh.shape["fsdp"], mesh.shape["seq"]),
        mesh=mesh,
        in_specs=placed,
        out_specs=(P(("fsdp", "seq"), None), P(("fsdp", "seq"), None)),
        check_vma=False,
    )
```

```python
import functools

import jax
import jax.numpy as jnp
from jax import lax
from jax.experimental import pallas as pl
from jax.experimental.pallas import tpu as pltpu
from jax.sharding import PartitionSpec as P

BF16, F32 = jnp.bfloat16, jnp.float32


def dot_t(left, right):
    return lax.dot_general(left, right, (((1,), (1,)), ((), ())), preferred_element_type=F32)


def dot(left, right):
    return jnp.dot(left, right, preferred_element_type=F32)


def forward(gate_pre, up_pre, mask):
    logistic = 1.0 / (1.0 + jnp.exp(-gate_pre))
    activated = gate_pre * logistic * mask
    return activated * up_pre, mask * up_pre * logistic * (1.0 + gate_pre * (1.0 - logistic)), activated


def factor_kernel(own_ref, twin_ref, mask_ref, factor_ref):
    q = mask_ref.shape[1]
    gate_pre, up_pre = (own_ref[:, i * q : (i + 1) * q] + twin_ref[:, i * q : (i + 1) * q].astype(F32) for i in range(2))
    _, factor_ref[:, :q], factor_ref[:, q:] = forward(gate_pre, up_pre, mask_ref[...])


def factors(own, twin, mask):
    rows, wide = own.shape
    q = wide // 2
    if q % 128:
        pre = own + twin.astype(F32)
        return jnp.concatenate(forward(pre[:, :q], pre[:, q:], mask)[1:], axis=1)
    tile = rows // 4
    block = lambda columns: pl.BlockSpec((tile, columns), lambda i: (i, 0))
    return pl.pallas_call(
        factor_kernel,
        grid=(4,),
        in_specs=[block(wide), block(wide), block(q)],
        out_specs=block(wide),
        out_shape=jax.ShapeDtypeStruct((rows, wide), F32),
        compiler_params=pltpu.CompilerParams(vmem_limit_bytes=32 * 2**20),
        cost_estimate=pl.CostEstimate(flops=0, bytes_accessed=300 * 2**20, transcendentals=0),
    )(own, twin, mask)


def pick_kernel(nf, kept, width, layer_ref, keep_ref, gate, up, down, *rest):
    sends, (down_out, keep_out) = rest[:nf], rest[nf : nf + 2]
    chosen, stage, down_stage, in_sems, out_sems = rest[nf + 2 :]
    tasks, blocks = keep_ref.shape
    for slot in range(kept):
        chosen[slot] = 0
    live = jnp.int32(0)
    flags = []
    for b in range(blocks):
        alive = keep_ref[0, b]
        for t in range(1, tasks):
            alive = jnp.maximum(alive, keep_ref[t, b])
        flags.append(alive)

        @pl.when((alive > 0) & (live < kept))
        def _(live=live, b=b):
            chosen[live] = b

        live = live + alive
    for b in range(blocks):

        @pl.when((flags[b] == 0) & (live < kept))
        def _(live=live, b=b):
            chosen[live] = b

        live = live + (1 - flags[b])
    layer = layer_ref[0]
    per = kept // nf
    arrivals = []

    def fetch(source, target):
        copy = pltpu.make_async_copy(source, target, in_sems.at[len(arrivals)])
        arrivals.append(copy)
        copy.start()

    order = [(p + 1) % nf for p in range(nf)]
    for p in order:
        dest = lax.bitwise_xor(layer, p)
        for i in range(per):
            block = pl.ds(pl.multiple_of(chosen[dest * per + i] * width, width), width)
            for half, source in enumerate((gate, up)):
                fetch(source.at[:, block], stage.at[p, :, pl.ds((half * per + i) * width, width)])
    for slot in range(kept):
        block = pl.ds(pl.multiple_of(chosen[slot] * width, width), width)
        fetch(down.at[block, :], down_stage.at[pl.ds(slot * width, width), :])
    for slot in range(kept):
        for t in range(tasks):
            keep_out[t, slot] = keep_ref[t, chosen[slot]]
    leaving = []
    for place, p in enumerate(order):
        for copy in arrivals[place * 2 * per : (place + 1) * 2 * per]:
            copy.wait()
        leaving.append(pltpu.make_async_copy(stage.at[p], sends[p], out_sems.at[p]))
        leaving[-1].start()
    for copy in arrivals[2 * kept :]:
        copy.wait()
    leaving.append(pltpu.make_async_copy(down_stage, down_out, out_sems.at[nf]))
    leaving[-1].start()
    for copy in leaving:
        copy.wait()


def pick(nf, f, keep_mask, gate_weight, up_weight, down_weight):
    tasks, blocks = keep_mask.shape
    deep, local_width = gate_weight.shape
    width = local_width // blocks
    kept = blocks * 4 // 7
    hidden = kept * width
    q = hidden // nf
    if kept % nf == 0:
        out = pl.pallas_call(
            functools.partial(pick_kernel, nf, kept, width),
            in_specs=[pl.BlockSpec(memory_space=pltpu.SMEM)] * 2 + [pl.BlockSpec(memory_space=pl.ANY)] * 3,
            out_specs=[pl.BlockSpec(memory_space=pl.ANY)] * (nf + 1) + [pl.BlockSpec(memory_space=pltpu.SMEM)],
            out_shape=[jax.ShapeDtypeStruct((deep, 2 * q), BF16)] * nf
            + [jax.ShapeDtypeStruct((hidden, down_weight.shape[1]), BF16), jax.ShapeDtypeStruct((tasks, kept), jnp.int32)],
            scratch_shapes=[
                pltpu.SMEM((kept,), jnp.int32),
                pltpu.VMEM((nf, deep, 2 * q), BF16),
                pltpu.VMEM((hidden, down_weight.shape[1]), BF16),
                pltpu.SemaphoreType.DMA((3 * kept,)),
                pltpu.SemaphoreType.DMA((nf + 1,)),
            ],
            compiler_params=pltpu.CompilerParams(vmem_limit_bytes=56 * 2**20),
            cost_estimate=pl.CostEstimate(flops=0, bytes_accessed=12 * deep * hidden, transcendentals=0),
        )(f.reshape(1), keep_mask, gate_weight, up_weight, down_weight)
        return out[:nf], out[nf], out[nf + 1]
    alive = jnp.max(keep_mask, axis=0)
    chosen = jnp.argsort((1 - alive) * blocks + jnp.arange(blocks, dtype=jnp.int32))[:kept]
    gate_pick, up_pick = (
        jnp.take(w.reshape(deep, blocks, width), chosen, axis=1).reshape(deep, hidden) for w in (gate_weight, up_weight)
    )
    down_pick = jnp.take(down_weight.reshape(blocks, width, -1), chosen, axis=0).reshape(hidden, -1)
    sends = [
        jnp.concatenate([lax.dynamic_slice_in_dim(w, (f ^ p) * q, q, 1) for w in (gate_pick, up_pick)], axis=1)
        for p in range(nf)
    ]
    return sends, down_pick, jnp.take(keep_mask, chosen, axis=1)


after = lax.optimization_barrier


def across(piece, p, n):
    return lax.ppermute(piece, "fsdp", [(i, i ^ p) for i in range(n)]) if p else piece


def in_order(pieces, f):
    stacked = jnp.zeros((len(pieces), *pieces[0].shape), pieces[0].dtype)
    for p, piece in enumerate(pieces):
        stacked = lax.dynamic_update_index_in_dim(stacked, piece, f ^ p, 0)
    return stacked


def line_steps(unit, n, axis, me):
    up = down = None
    for k in range(1, n):
        ahead, behind = unit(jnp.clip(me + n - k, 0, n - 1)), unit(jnp.clip(me - n + k, 0, n - 1))
        if k > 1:
            ahead, behind = ahead + up.astype(F32), behind + down.astype(F32)
        up = lax.ppermute(ahead.astype(BF16), axis, [(i, i + 1) for i in range(k)])
        down = lax.ppermute(behind.astype(BF16), axis, [(i, i - 1) for i in range(n - k, n)])
        up, down = yield up, down
    return unit(me) + up.astype(F32) + down.astype(F32)


def layers_sum(unit, n, me):
    arrived = [across(unit(me ^ p).astype(BF16), p, n) for p in range(1, n)]
    arrived = yield arrived
    total = unit(me)
    for piece in arrived:
        total = total + piece.astype(F32)
    return total


def finish(steps, arrived):
    try:
        while True:
            arrived = steps.send(arrived)
    except StopIteration as end:
        return end.value


def assemble_kernel(places, *refs):
    out = refs[-1]
    for row, column, part, first, count in places:
        width = refs[part].shape[1]
        out[pl.ds(row, count), pl.ds(column, width)] = refs[part][pl.ds(first, count), :]


def assemble(arrays, places, shape):
    if shape[0] * shape[1] > 2**23:
        return jnp.concatenate(arrays)
    return pl.pallas_call(
        functools.partial(assemble_kernel, places),
        in_specs=[pl.BlockSpec(memory_space=pltpu.VMEM)] * len(arrays),
        out_specs=pl.BlockSpec(memory_space=pltpu.VMEM),
        out_shape=jax.ShapeDtypeStruct(shape, BF16),
        compiler_params=pltpu.CompilerParams(vmem_limit_bytes=32 * 2**20),
    )(*arrays)


def stack_rows(arrays):
    rows, columns = arrays[0].shape
    return assemble(arrays, [(d * rows, 0, d, 0, rows) for d in range(len(arrays))], (len(arrays) * rows, columns))


def seq_gather(x, n):
    return [x] + [lax.ppermute(x, "seq", [(i, i ^ d) for i in range(n)]) for d in range(1, n)]


def layer_scatter(rows, weight, n):
    pieces = jnp.split(rows, n)
    count = n.bit_length() - 1
    halves = jnp.split(weight, 2)
    held = [list(range(n)) for _ in halves]
    got = [{d: [] for d in range(n)} for _ in halves]
    for step in range(count):
        for side, bit in enumerate((step, count - 1 - step)):
            sent = [d for d in held[side] if d >> bit & 1]
            held[side] = [d for d in held[side] if not d >> bit & 1]
            part = dot_t(jnp.concatenate([pieces[d] for d in sent]), halves[side])
            for piece in zip(*(got[side][d] for d in sent)):
                part = part + jnp.concatenate(piece).astype(F32)
            arrived = lax.ppermute(part.astype(BF16), "seq", [(i, i ^ (2 << bit)) for i in range(2 * n)])
            for d, piece in zip(sent, jnp.split(arrived, len(sent))):
                got[side][d ^ (1 << bit)].append(piece)
        got = yield got
    totals = []
    for side, half in enumerate(halves):
        total = dot_t(pieces[0], half)
        for piece in got[side][0]:
            total = total + piece.astype(F32)
        totals.append(total)
    return jnp.concatenate(totals, axis=1)


def local(nf, ns, tokens, grad_out, gate_weight, up_weight, down_weight, keep_mask, task_ids):
    f, s = lax.axis_index("fsdp"), lax.axis_index("seq")
    core, chip, chips = s & 1, s >> 1, ns // 2
    rows, wide = tokens.shape
    deep, half = wide // nf, wide // 2
    every = nf * ns * rows
    swap = [(i, i ^ 1) for i in range(ns)]

    with jax.named_scope("pick"):
        sends, down_pick, keep_pick = pick(nf, f, keep_mask, gate_weight, up_weight, down_weight)
    hidden_width = down_pick.shape[0]
    q = hidden_width // nf

    with jax.named_scope("grad_rows"):
        extra = jnp.zeros((8 * deep,), BF16).at[: ns * rows].set(task_ids.astype(BF16)).reshape(8, deep)
        pieces = [
            jnp.concatenate([lax.dynamic_slice_in_dim(grad_out, (f ^ p) * deep, deep, 1), extra]) for p in range(nf)
        ]
        grads = in_order([across(piece, p, nf) for p, piece in enumerate(pieces)], f)
        ids = grads[:, rows:].reshape(nf, 8 * deep)[:, : ns * rows].reshape(nf, chips, 2 * rows)
        ids = ids.transpose(1, 0, 2).reshape(every)
        grads, sends = after((grads[:, :rows].reshape(nf * rows, deep), sends))
        got = [sends[0], *(across(sends[p], p, nf) for p in (1, 2))]
        grads = seq_gather(grads, ns)

    with jax.named_scope("token_rows"):
        own_rows = lax.dynamic_slice_in_dim(tokens, core * half, half, 1)
        twin_rows = lax.ppermute(lax.dynamic_slice_in_dim(tokens, (1 - core) * half, half, 1), "seq", swap)
        token_rows = jnp.where(
            core == 0, jnp.concatenate([own_rows, twin_rows]), jnp.concatenate([twin_rows, own_rows])
        )
        token_rows = lax.all_gather(token_rows, "fsdp", axis=0, tiled=True)
        token_rows, grads, got, sends = after((token_rows, grads, got, sends))
        same_core = [[i for i in range(ns) if i & 1 == c] for c in range(2)]
        token_rows = lax.all_gather(token_rows, "seq", axis=0, tiled=True, axis_index_groups=same_core)

    with jax.named_scope("hidden_grad"):
        got += [across(sends[p], p, nf) for p in range(3, nf)]
        part = dot_t(stack_rows(grads[::2] + grads[1::2]), down_pick)
        steps = line_steps(lambda j: lax.dynamic_slice_in_dim(part, j * q, q, 1), nf, "fsdp", f)
        arrived, got = after((next(steps), got))

    with jax.named_scope("weights"):
        weight = in_order(got, f).reshape(wide, 2 * q)
        mine = lax.dynamic_slice_in_dim(weight, core * half, half, 0)
        other = lax.ppermute(lax.dynamic_slice_in_dim(weight, (1 - core) * half, half, 0), "seq", swap)
        both_weight = jnp.concatenate([mine, other], axis=1)

    with jax.named_scope("mask"):
        tasks, kept = keep_pick.shape
        onehot = (ids[:, None] == jnp.arange(tasks, dtype=jnp.int32)[None, :]).astype(BF16)
        keep_columns = jnp.repeat(keep_pick.astype(BF16), hidden_width // kept, axis=1)
        mask = dot(onehot, lax.dynamic_slice_in_dim(keep_columns, f * q, q, 1))

    with jax.named_scope("forward"):
        pre = dot(token_rows, both_weight)
        arrived, pre = after((steps.send(arrived), pre))
        own, twin = pre[:, : 2 * q], lax.ppermute(pre[:, 2 * q :].astype(BF16), "seq", swap)
        pre = own + twin.astype(F32)
        hidden = forward(pre[:, :q], pre[:, q:], mask)[0]
        hidden = hidden.astype(BF16).reshape(chips, nf, 2, rows, q).transpose(0, 2, 1, 3, 4).reshape(every, q)
        hidden, own = after((hidden, own))
        hidden_all = lax.all_gather(hidden, "fsdp", axis=1, tiled=True)
        factor = factors(own, twin, mask)
        if nf > 3:
            arrived = steps.send(arrived)
        factor = factor.reshape(chips, nf, 2, rows, 2 * q)
        factor = jnp.stack([lax.dynamic_index_in_dim(factor, chip ^ d, 0, keepdims=False) for d in range(chips)])
        arrived, factor = after((arrived, factor))
        hidden_grad = finish(steps, arrived)

    with jax.named_scope("input_grad"):
        hidden_grad = hidden_grad.reshape(2, every // 2, q)
        own = []
        for c in range(2):
            chunk = lax.dynamic_index_in_dim(hidden_grad, c ^ core, 0, keepdims=False)
            scale = factor[:, :, c].reshape(every // 2, 2 * q)
            own.append((scale * jnp.concatenate([chunk, chunk], axis=1)).astype(BF16))
        both = [jnp.concatenate([own[c], lax.ppermute(own[c], "seq", swap)], axis=1) for c in range(2)]

        def over_layers(part):
            part = part.reshape(nf, rows, half)
            return layers_sum(lambda j: lax.dynamic_index_in_dim(part, j, 0, keepdims=False), nf, f)

        steps = chips.bit_length() - 1
        first = layer_scatter(both[0], both_weight, chips)
        arrived = next(first)
        for _ in range(steps - 1):
            arrived = first.send(arrived)
        arrived, both[1] = after((arrived, both[1]))
        second = layer_scatter(both[1], both_weight, chips)
        part = finish(first, arrived)
        waiting, hidden_all, part = after((next(second), hidden_all, part))
        for _ in range(steps - 1):
            waiting = second.send(waiting)
        first = over_layers(part)
        arrived, waiting = after((next(first), waiting))
        second = over_layers(finish(second, waiting))
        totals = [finish(first, arrived).astype(BF16), finish(second, next(second)).astype(BF16)]
        here = jnp.where(core == 0, totals[0], totals[1])
        there = lax.ppermute(jnp.where(core == 0, totals[1], totals[0]), "seq", swap)
        input_grad = jnp.where(
            core == 0, jnp.concatenate([here, there], axis=1), jnp.concatenate([there, here], axis=1)
        )

    with jax.named_scope("layer_out"):
        out_part = dot(hidden_all, down_pick).astype(BF16)
        out = lax.psum_scatter(out_part, "seq", scatter_dimension=0, tiled=True)
        out = lax.all_to_all(out.reshape(nf, rows, deep), "fsdp", 0, 0, tiled=False)
        layer_out = out.transpose(1, 0, 2).reshape(rows, wide)
    return layer_out, input_grad


def solution(mesh):
    placed = (
        P(("fsdp", "seq"), None),
        P(("fsdp", "seq"), None),
        P("fsdp", "seq"),
        P("fsdp", "seq"),
        P("seq", "fsdp"),
        P(None, "seq"),
        P("fsdp"),
    )
    return jax.shard_map(
        functools.partial(local, mesh.shape["fsdp"], mesh.shape["seq"]),
        mesh=mesh,
        in_specs=placed,
        out_specs=(P(("fsdp", "seq"), None), P(("fsdp", "seq"), None)),
        check_vma=False,
    )
```

```python
import functools

import jax
import jax.numpy as jnp
from jax import lax
from jax.experimental import pallas as pl
from jax.experimental.pallas import tpu as pltpu
from jax.sharding import PartitionSpec as P

BF16, F32 = jnp.bfloat16, jnp.float32


def dot_t(left, right):
    return lax.dot_general(left, right, (((1,), (1,)), ((), ())), preferred_element_type=F32)


def dot(left, right):
    return jnp.dot(left, right, preferred_element_type=F32)


def forward(gate_pre, up_pre, mask):
    logistic = 1.0 / (1.0 + jnp.exp(-gate_pre))
    activated = gate_pre * logistic * mask
    return activated * up_pre, mask * up_pre * logistic * (1.0 + gate_pre * (1.0 - logistic)), activated


def factor_kernel(own_ref, twin_ref, mask_ref, factor_ref):
    q = mask_ref.shape[1]
    gate_pre, up_pre = (own_ref[:, i * q : (i + 1) * q] + twin_ref[:, i * q : (i + 1) * q].astype(F32) for i in range(2))
    _, factor_ref[:, :q], factor_ref[:, q:] = forward(gate_pre, up_pre, mask_ref[...])


def factors(own, twin, mask):
    rows, wide = own.shape
    q = wide // 2
    if q % 128:
        pre = own + twin.astype(F32)
        return jnp.concatenate(forward(pre[:, :q], pre[:, q:], mask)[1:], axis=1)
    tile = rows // 4
    block = lambda columns: pl.BlockSpec((tile, columns), lambda i: (i, 0))
    return pl.pallas_call(
        factor_kernel,
        grid=(4,),
        in_specs=[block(wide), block(wide), block(q)],
        out_specs=block(wide),
        out_shape=jax.ShapeDtypeStruct((rows, wide), F32),
        compiler_params=pltpu.CompilerParams(vmem_limit_bytes=32 * 2**20),
        cost_estimate=pl.CostEstimate(flops=0, bytes_accessed=300 * 2**20, transcendentals=0),
    )(own, twin, mask)


def pick_kernel(nf, kept, width, layer_ref, keep_ref, gate, up, down, *rest):
    sends, (down_out, keep_out) = rest[:nf], rest[nf : nf + 2]
    chosen, stage, down_stage, in_sems, out_sems = rest[nf + 2 :]
    tasks, blocks = keep_ref.shape
    for slot in range(kept):
        chosen[slot] = 0
    live = jnp.int32(0)
    flags = []
    for b in range(blocks):
        alive = keep_ref[0, b]
        for t in range(1, tasks):
            alive = jnp.maximum(alive, keep_ref[t, b])
        flags.append(alive)

        @pl.when((alive > 0) & (live < kept))
        def _(live=live, b=b):
            chosen[live] = b

        live = live + alive
    for b in range(blocks):

        @pl.when((flags[b] == 0) & (live < kept))
        def _(live=live, b=b):
            chosen[live] = b

        live = live + (1 - flags[b])
    layer = layer_ref[0]
    per = kept // nf
    arrivals = []

    def fetch(source, target):
        copy = pltpu.make_async_copy(source, target, in_sems.at[len(arrivals)])
        arrivals.append(copy)
        copy.start()

    order = [(p + 1) % nf for p in range(nf)]
    for p in order:
        dest = lax.bitwise_xor(layer, p)
        for i in range(per):
            block = pl.ds(pl.multiple_of(chosen[dest * per + i] * width, width), width)
            for half, source in enumerate((gate, up)):
                fetch(source.at[:, block], stage.at[p, :, pl.ds((half * per + i) * width, width)])
    for slot in range(kept):
        block = pl.ds(pl.multiple_of(chosen[slot] * width, width), width)
        fetch(down.at[block, :], down_stage.at[pl.ds(slot * width, width), :])
    for slot in range(kept):
        for t in range(tasks):
            keep_out[t, slot] = keep_ref[t, chosen[slot]]
    leaving = []
    for place, p in enumerate(order):
        for copy in arrivals[place * 2 * per : (place + 1) * 2 * per]:
            copy.wait()
        leaving.append(pltpu.make_async_copy(stage.at[p], sends[p], out_sems.at[p]))
        leaving[-1].start()
    for copy in arrivals[2 * kept :]:
        copy.wait()
    leaving.append(pltpu.make_async_copy(down_stage, down_out, out_sems.at[nf]))
    leaving[-1].start()
    for copy in leaving:
        copy.wait()


def pick(nf, f, keep_mask, gate_weight, up_weight, down_weight):
    tasks, blocks = keep_mask.shape
    deep, local_width = gate_weight.shape
    width = local_width // blocks
    kept = blocks * 4 // 7
    hidden = kept * width
    q = hidden // nf
    if kept % nf == 0:
        out = pl.pallas_call(
            functools.partial(pick_kernel, nf, kept, width),
            in_specs=[pl.BlockSpec(memory_space=pltpu.SMEM)] * 2 + [pl.BlockSpec(memory_space=pl.ANY)] * 3,
            out_specs=[pl.BlockSpec(memory_space=pl.ANY)] * (nf + 1) + [pl.BlockSpec(memory_space=pltpu.SMEM)],
            out_shape=[jax.ShapeDtypeStruct((deep, 2 * q), BF16)] * nf
            + [jax.ShapeDtypeStruct((hidden, down_weight.shape[1]), BF16), jax.ShapeDtypeStruct((tasks, kept), jnp.int32)],
            scratch_shapes=[
                pltpu.SMEM((kept,), jnp.int32),
                pltpu.VMEM((nf, deep, 2 * q), BF16),
                pltpu.VMEM((hidden, down_weight.shape[1]), BF16),
                pltpu.SemaphoreType.DMA((3 * kept,)),
                pltpu.SemaphoreType.DMA((nf + 1,)),
            ],
            compiler_params=pltpu.CompilerParams(vmem_limit_bytes=56 * 2**20),
            cost_estimate=pl.CostEstimate(flops=0, bytes_accessed=12 * deep * hidden, transcendentals=0),
        )(f.reshape(1), keep_mask, gate_weight, up_weight, down_weight)
        return out[:nf], out[nf], out[nf + 1]
    alive = jnp.max(keep_mask, axis=0)
    chosen = jnp.argsort((1 - alive) * blocks + jnp.arange(blocks, dtype=jnp.int32))[:kept]
    gate_pick, up_pick = (
        jnp.take(w.reshape(deep, blocks, width), chosen, axis=1).reshape(deep, hidden) for w in (gate_weight, up_weight)
    )
    down_pick = jnp.take(down_weight.reshape(blocks, width, -1), chosen, axis=0).reshape(hidden, -1)
    sends = [
        jnp.concatenate([lax.dynamic_slice_in_dim(w, (f ^ p) * q, q, 1) for w in (gate_pick, up_pick)], axis=1)
        for p in range(nf)
    ]
    return sends, down_pick, jnp.take(keep_mask, chosen, axis=1)


after = lax.optimization_barrier


def across(piece, p, n):
    return lax.ppermute(piece, "fsdp", [(i, i ^ p) for i in range(n)]) if p else piece


def in_order(pieces, f):
    stacked = jnp.zeros((len(pieces), *pieces[0].shape), pieces[0].dtype)
    for p, piece in enumerate(pieces):
        stacked = lax.dynamic_update_index_in_dim(stacked, piece, f ^ p, 0)
    return stacked


def line_steps(unit, n, axis, me):
    up = down = None
    for k in range(1, n):
        ahead, behind = unit(jnp.clip(me + n - k, 0, n - 1)), unit(jnp.clip(me - n + k, 0, n - 1))
        if k > 1:
            ahead, behind = ahead + up.astype(F32), behind + down.astype(F32)
        up = lax.ppermute(ahead.astype(BF16), axis, [(i, i + 1) for i in range(k)])
        down = lax.ppermute(behind.astype(BF16), axis, [(i, i - 1) for i in range(n - k, n)])
        up, down = yield up, down
    return unit(me) + up.astype(F32) + down.astype(F32)


def layers_sum(unit, n, me):
    arrived = [across(unit(me ^ p).astype(BF16), p, n) for p in range(1, n)]
    arrived = yield arrived
    total = unit(me)
    for piece in arrived:
        total = total + piece.astype(F32)
    return total


def finish(steps, arrived):
    try:
        while True:
            arrived = steps.send(arrived)
    except StopIteration as end:
        return end.value


def assemble_kernel(places, *refs):
    out = refs[-1]
    for row, column, part, first, count in places:
        width = refs[part].shape[1]
        out[pl.ds(row, count), pl.ds(column, width)] = refs[part][pl.ds(first, count), :]


def assemble(arrays, places, shape):
    if shape[0] * shape[1] > 2**23:
        return jnp.concatenate(arrays)
    return pl.pallas_call(
        functools.partial(assemble_kernel, places),
        in_specs=[pl.BlockSpec(memory_space=pltpu.VMEM)] * len(arrays),
        out_specs=pl.BlockSpec(memory_space=pltpu.VMEM),
        out_shape=jax.ShapeDtypeStruct(shape, BF16),
        compiler_params=pltpu.CompilerParams(vmem_limit_bytes=32 * 2**20),
    )(*arrays)


def stack_rows(arrays):
    rows, columns = arrays[0].shape
    return assemble(arrays, [(d * rows, 0, d, 0, rows) for d in range(len(arrays))], (len(arrays) * rows, columns))


def seq_gather(x, n):
    return [x] + [lax.ppermute(x, "seq", [(i, i ^ d) for i in range(n)]) for d in range(1, n)]


def layer_scatter(rows, weight, n):
    pieces = jnp.split(rows, n)
    count = n.bit_length() - 1
    halves = jnp.split(weight, 2)
    held = [list(range(n)) for _ in halves]
    got = [{d: [] for d in range(n)} for _ in halves]
    for step in range(count):
        for side, bit in enumerate((step, count - 1 - step)):
            sent = [d for d in held[side] if d >> bit & 1]
            held[side] = [d for d in held[side] if not d >> bit & 1]
            part = dot_t(jnp.concatenate([pieces[d] for d in sent]), halves[side])
            for piece in zip(*(got[side][d] for d in sent)):
                part = part + jnp.concatenate(piece).astype(F32)
            arrived = lax.ppermute(part.astype(BF16), "seq", [(i, i ^ (2 << bit)) for i in range(2 * n)])
            for d, piece in zip(sent, jnp.split(arrived, len(sent))):
                got[side][d ^ (1 << bit)].append(piece)
        got = yield got
    totals = []
    for side, half in enumerate(halves):
        total = dot_t(pieces[0], half)
        for piece in got[side][0]:
            total = total + piece.astype(F32)
        totals.append(total)
    return jnp.concatenate(totals, axis=1)


def local(nf, ns, tokens, grad_out, gate_weight, up_weight, down_weight, keep_mask, task_ids):
    f, s = lax.axis_index("fsdp"), lax.axis_index("seq")
    core, chip, chips = s & 1, s >> 1, ns // 2
    rows, wide = tokens.shape
    deep, half = wide // nf, wide // 2
    every = nf * ns * rows
    swap = [(i, i ^ 1) for i in range(ns)]

    with jax.named_scope("pick"):
        sends, down_pick, keep_pick = pick(nf, f, keep_mask, gate_weight, up_weight, down_weight)
    hidden_width = down_pick.shape[0]
    q = hidden_width // nf

    with jax.named_scope("grad_rows"):
        extra = jnp.zeros((8 * deep,), BF16).at[: ns * rows].set(task_ids.astype(BF16)).reshape(8, deep)
        pieces = [
            jnp.concatenate([lax.dynamic_slice_in_dim(grad_out, (f ^ p) * deep, deep, 1), extra]) for p in range(nf)
        ]
        grads = in_order([across(piece, p, nf) for p, piece in enumerate(pieces)], f)
        ids = grads[:, rows:].reshape(nf, 8 * deep)[:, : ns * rows].reshape(nf, chips, 2 * rows)
        ids = ids.transpose(1, 0, 2).reshape(every)
        grads, sends = after((grads[:, :rows].reshape(nf * rows, deep), sends))
        got = [sends[0], *(across(sends[p], p, nf) for p in (1, 2))]
        grads = seq_gather(grads, ns)

    with jax.named_scope("token_rows"):
        own_rows = lax.dynamic_slice_in_dim(tokens, core * half, half, 1)
        twin_rows = lax.ppermute(lax.dynamic_slice_in_dim(tokens, (1 - core) * half, half, 1), "seq", swap)
        token_rows = jnp.where(
            core == 0, jnp.concatenate([own_rows, twin_rows]), jnp.concatenate([twin_rows, own_rows])
        )
        token_rows = lax.all_gather(token_rows, "fsdp", axis=0, tiled=True)
        token_rows, grads, got, sends = after((token_rows, grads, got, sends))
        same_core = [[i for i in range(ns) if i & 1 == c] for c in range(2)]
        token_rows = lax.all_gather(token_rows, "seq", axis=0, tiled=True, axis_index_groups=same_core)

    with jax.named_scope("hidden_grad"):
        got += [across(sends[p], p, nf) for p in range(3, nf)]
        part = dot_t(stack_rows(grads[::2] + grads[1::2]), down_pick)
        steps = line_steps(lambda j: lax.dynamic_slice_in_dim(part, j * q, q, 1), nf, "fsdp", f)
        arrived, got = after((next(steps), got))

    with jax.named_scope("weights"):
        weight = in_order(got, f).reshape(wide, 2 * q)
        mine = lax.dynamic_slice_in_dim(weight, core * half, half, 0)
        other = lax.ppermute(lax.dynamic_slice_in_dim(weight, (1 - core) * half, half, 0), "seq", swap)
        both_weight = jnp.concatenate([mine, other], axis=1)

    with jax.named_scope("mask"):
        tasks, kept = keep_pick.shape
        onehot = (ids[:, None] == jnp.arange(tasks, dtype=jnp.int32)[None, :]).astype(BF16)
        keep_columns = jnp.repeat(keep_pick.astype(BF16), hidden_width // kept, axis=1)
        mask = dot(onehot, lax.dynamic_slice_in_dim(keep_columns, f * q, q, 1))

    with jax.named_scope("forward"):
        pre = dot(token_rows, both_weight)
        arrived, pre = after((steps.send(arrived), pre))
        own, twin = pre[:, : 2 * q], lax.ppermute(pre[:, 2 * q :].astype(BF16), "seq", swap)
        pre = own + twin.astype(F32)
        hidden = forward(pre[:, :q], pre[:, q:], mask)[0]
        hidden = hidden.astype(BF16).reshape(chips, nf, 2, rows, q).transpose(0, 2, 1, 3, 4).reshape(every, q)
        hidden, own = after((hidden, own))
        hidden_all = lax.all_gather(hidden, "fsdp", axis=1, tiled=True)
        factor = factors(own, twin, mask)
        if nf > 3:
            arrived = steps.send(arrived)
        factor = factor.reshape(chips, nf, 2, rows, 2 * q)
        factor = jnp.stack([lax.dynamic_index_in_dim(factor, chip ^ d, 0, keepdims=False) for d in range(chips)])
        arrived, factor = after((arrived, factor))
        hidden_grad = finish(steps, arrived)

    with jax.named_scope("input_grad"):
        hidden_grad = hidden_grad.reshape(2, every // 2, q)
        own = []
        for c in range(2):
            chunk = lax.dynamic_index_in_dim(hidden_grad, c ^ core, 0, keepdims=False)
            scale = factor[:, :, c].reshape(every // 2, 2 * q)
            own.append((scale * jnp.concatenate([chunk, chunk], axis=1)).astype(BF16))
        both = [jnp.concatenate([own[c], lax.ppermute(own[c], "seq", swap)], axis=1) for c in range(2)]

        def over_layers(part):
            part = part.reshape(nf, rows, half)
            return layers_sum(lambda j: lax.dynamic_index_in_dim(part, j, 0, keepdims=False), nf, f)

        steps = chips.bit_length() - 1
        first = layer_scatter(both[0], both_weight, chips)
        arrived = next(first)
        for _ in range(steps - 1):
            arrived = first.send(arrived)
        arrived, both[1] = after((arrived, both[1]))
        second = layer_scatter(both[1], both_weight, chips)
        waiting, hidden_all = after((next(second), hidden_all))
        for _ in range(steps - 1):
            waiting = second.send(waiting)
        first = over_layers(finish(first, arrived))
        arrived, waiting = after((next(first), waiting))
        second = over_layers(finish(second, waiting))
        out_part = dot(hidden_all, down_pick).astype(BF16)
        out = lax.psum_scatter(out_part, "seq", scatter_dimension=0, tiled=True)
        waiting, out = after((next(second), out))
        totals = [finish(first, arrived).astype(BF16), finish(second, waiting).astype(BF16)]
        here = jnp.where(core == 0, totals[0], totals[1])
        there = lax.ppermute(jnp.where(core == 0, totals[1], totals[0]), "seq", swap)
        input_grad = jnp.where(
            core == 0, jnp.concatenate([here, there], axis=1), jnp.concatenate([there, here], axis=1)
        )

    with jax.named_scope("layer_out"):
        out = lax.all_to_all(out.reshape(nf, rows, deep), "fsdp", 0, 0, tiled=False)
        layer_out = out.transpose(1, 0, 2).reshape(rows, wide)
    return layer_out, input_grad


def solution(mesh):
    placed = (
        P(("fsdp", "seq"), None),
        P(("fsdp", "seq"), None),
        P("fsdp", "seq"),
        P("fsdp", "seq"),
        P("seq", "fsdp"),
        P(None, "seq"),
        P("fsdp"),
    )
    return jax.shard_map(
        functools.partial(local, mesh.shape["fsdp"], mesh.shape["seq"]),
        mesh=mesh,
        in_specs=placed,
        out_specs=(P(("fsdp", "seq"), None), P(("fsdp", "seq"), None)),
        check_vma=False,
    )
```
